32 devices in a mesh: grp: 2 (over y), store: 8 (over z, core), tp: 2 (over x).
Axes of the slice: x: 2, y: 2, z: 4, core: 2. Of those that a mesh axis runs over, the one named last changes fastest.
Arguments:
- tokens: bfloat16 [10240, 8192], P(('grp', 'store'), 'tp'), parts along dimension 0, may hold values from -6 to 6
- value_matrix: bfloat16 [8192, 1024], P('tp'), may hold values from -0.0625 to 0.0625
- adapter_down_matrix: bfloat16 [64, 8192, 128], P(('grp', 'store'), 'tp'), parts along dimension 0, may hold values from -0.0625 to 0.0625
- adapter_up_matrix: bfloat16 [64, 128, 1024], P(('grp', 'store'), None, 'tp'), parts along dimension 0, may hold values from -0.5 to 0.5
- adapter_rank_list: int32 [64], P('grp'), parts along dimension 0, may hold values from 16 to 128
- requests: int32 [16, 4], P(('grp', 'store')), parts along dimension 0, may hold values from 0 to 31, as said below
- segment_row_lengths: int32 [16, 4], P(('grp', 'store')), parts along dimension 0, may hold values from 1 to 320, 640 in all within a row
Outputs:
- adapted_values: bfloat16 [10240, 1024], P(('grp', 'store'), 'tp'), parts along dimension 0
The draws below stay inside these ranges and needn't reach their ends.
There are 2 independent parts, one for each index of `grp`. The reference program is written for one: setup_inputs(seed, part) draws one part's arguments, and reference() takes and returns one part's arrays. A program takes and returns all parts, laid end to end along the dimension named above; an argument that names none is the same for every part. Nothing has to cross between parts.
Inputs may be any that keep to these rules, and one draw needn't show every extreme that they name: `requests`: entry (j, s) names the adapter of segment s of instance j; adapter a is stored at index a // 4 of store, and the 4 adapters of one instance are stored on 4 different indices of store. `segment_row_lengths`: each instance's 4 lengths sum to 640.
All inputs are finite; a program needn't handle non-finite values.
Results may differ from the reference program's by a relative error of at most 0.0034.
Values may be sent and summed in bfloat16 or wider, within the bound.
A program may use at most 128 MiB of HBM per device.

```python
import math
import jax
import jax.numpy as jnp
import numpy as np
from jax import lax

MODEL_WIDTH = 8192
VALUE_OUT_WIDTH = 1024
LARGEST_RANK = 128
ROWS_DEV = 640
ADP_DEV = 4
ADAPTERS_USED = 4
SEGMENT_ROWS_TOP = 320
ADAPTERS_STORED = 32
ROWS = 5120
N_STORE = 8


def draw_requests(key, part):
    key = jax.random.fold_in(key, 11)
    subkeys = jax.random.split(key, 2)
    row_keys = jax.random.split(subkeys[0], N_STORE)

    def row_owners(row_key):
        return jax.random.permutation(row_key, N_STORE)[:ADAPTERS_USED]
    owners = jax.vmap(row_owners)(row_keys)
    local_ids = jax.random.randint(subkeys[1], (N_STORE, ADAPTERS_USED), 0, ADP_DEV)
    return (owners * ADP_DEV + local_ids).astype(jnp.int32)


def with_ends(drawn, stream_key, least, top_value):
    extent = drawn.shape
    spot = [jax.random.randint(jax.random.fold_in(stream_key, axis), (), 0, extent[axis]) for axis in range(len(extent))]
    drawn = drawn.at[tuple(spot)].set(least)
    longest = extent.index(max(extent))
    spot[longest] = (spot[longest] + 1) % extent[longest]
    return drawn.at[tuple(spot)].set(top_value)


def block_scale(own_key, dims, shards, low, top_value):
    factor_of, own = 1.0, jax.random.fold_in(own_key, 6)
    for position, blocks in shards:
        steps = jnp.exp(jax.random.uniform(jax.random.fold_in(own, position), (blocks,), jnp.float32, low / len(shards), top_value / len(shards)))
        factor_of = factor_of * jnp.repeat(steps, dims[position] // blocks).reshape([-1 if axis == position else 1 for axis in range(len(dims))])
    return factor_of


def profile(amount, total, bound, skew):
    weights = [(1 << 20) // math.isqrt(rank ** skew) + 1 for rank in range(2, amount + 1)]
    spare, counts = total - bound - (amount - 1), [1] * (amount - 1)
    while spare > 0:
        candidates = [i for i in range(amount - 1) if counts[i] < bound]
        whole, budget = sum([weights[i] for i in candidates]), spare
        for i in candidates:
            extra = min(bound - counts[i], max(1, budget * weights[i] // whole), spare)
            counts[i] = counts[i] + extra
            spare = spare - extra
    return np.array([bound] + counts)


def ragged(own_key, amount, total, bound, slope):
    if amount == 2:
        one = jax.random.randint(own_key, (), max(1, total - bound), min(bound, total - 1) + 1)
        return jnp.stack([one, total - one])
    sizes = jnp.asarray(profile(amount, total, bound, slope), jnp.int32)
    couples = (amount - 1) // 2
    giver, sink = sizes[1:1 + 2 * couples:2], sizes[2:2 + 2 * couples:2]
    slack = jnp.minimum(giver - 1, bound - sink)
    moved = jax.random.randint(jax.random.fold_in(own_key, 1), (couples,), 0, 1 << 20) % (slack + 1)
    sizes = sizes.at[1:1 + 2 * couples:2].set(giver - moved).at[2:2 + 2 * couples:2].set(sink + moved)
    return sizes[jax.random.permutation(jax.random.fold_in(own_key, 2), amount)]


def normal_values(key, extent, width, bound, cuts=(), kind=jnp.bfloat16):
    entries = width * jax.random.normal(key, extent, jnp.float32)
    if cuts:
        entries = entries * block_scale(key, extent, cuts, -0.22, 0.18)
    return jnp.clip(entries, -bound, bound).astype(kind)


def setup_inputs(seed: int = 0, part: int = 0) -> dict:
    streams_of = jax.random.split(jax.random.key(seed), 8)
    part_splits = jax.random.split(jax.random.fold_in(streams_of[7], part), 8)
    tokens = normal_values(part_splits[0], (ROWS, MODEL_WIDTH), 1.0, 6.0, ((0, 8), (1, 2)))
    value_matrix = normal_values(streams_of[1], (MODEL_WIDTH, VALUE_OUT_WIDTH), MODEL_WIDTH ** -0.5, 0.0625, ((0, 2),))
    adapter_down_matrix = normal_values(part_splits[2], (ADAPTERS_STORED, MODEL_WIDTH, LARGEST_RANK), MODEL_WIDTH ** -0.5, 0.0625, ((0, 8), (1, 2)))
    adapter_up_matrix = normal_values(part_splits[3], (ADAPTERS_STORED, LARGEST_RANK, VALUE_OUT_WIDTH), LARGEST_RANK ** -0.5, 0.5, ((0, 8), (2, 2)))
    adapter_rank_list = with_ends(jax.random.randint(part_splits[4], (ADAPTERS_STORED,), LARGEST_RANK // 8, LARGEST_RANK + 1), jax.random.fold_in(part_splits[4], 1), LARGEST_RANK // 8, LARGEST_RANK).astype(jnp.int32)
    requests = draw_requests(jax.random.fold_in(jax.random.fold_in(streams_of[7], part), 71), part)
    segment_row_lengths = jax.vmap(lambda own: ragged(own, ADAPTERS_USED, ROWS_DEV, SEGMENT_ROWS_TOP, 2))(jax.random.split(part_splits[6], N_STORE)).reshape((N_STORE, ADAPTERS_USED)).astype(jnp.int32)
    return dict(tokens=tokens, value_matrix=value_matrix, adapter_down_matrix=adapter_down_matrix, adapter_up_matrix=adapter_up_matrix, adapter_rank_list=adapter_rank_list, requests=requests, segment_row_lengths=segment_row_lengths)


adapter_alpha = 32.0


def reference(tokens, value_matrix, adapter_down_matrix, adapter_up_matrix, adapter_rank_list, requests, segment_row_lengths):
    base_values = jnp.dot(tokens, value_matrix, preferred_element_type=jnp.float32)
    step_ids = jnp.arange(SEGMENT_ROWS_TOP, dtype=jnp.int32)
    row_ids = jnp.arange(ROWS_DEV, dtype=jnp.int32)
    column_ids = jnp.arange(LARGEST_RANK, dtype=jnp.int32)

    def instance_delta(packed):
        inst_rows, desired_identifiers, inst_lengths = packed
        starts = (jnp.cumsum(inst_lengths) - inst_lengths).astype(jnp.int32)
        window_index = jnp.minimum(starts[:, None] + step_ids[None, :], ROWS_DEV - 1).astype(jnp.int32)
        segment_spans = inst_rows[window_index].astype(jnp.float32)
        chosen_down = adapter_down_matrix[desired_identifiers].astype(jnp.float32)
        adapter_middle = jnp.einsum("kng,kgz->knz", segment_spans, chosen_down)
        chosen_ranks = adapter_rank_list[desired_identifiers]
        retained_columns = (column_ids[None, :] < chosen_ranks[:, None]).astype(jnp.float32)
        column_factors = retained_columns * (adapter_alpha / chosen_ranks.astype(jnp.float32))[:, None]
        scaled_update = (adapter_middle * column_factors[:, None, :]).astype(jnp.bfloat16)
        scaled_update = lax.optimization_barrier(scaled_update)
        chosen_up = adapter_up_matrix[desired_identifiers].astype(jnp.float32)
        adapter_update = jnp.einsum("poa,pal->pol", scaled_update.astype(jnp.float32), chosen_up)
        segment_piece = (jnp.sum((starts[None, :] <= row_ids[:, None]).astype(jnp.int32), axis=1) - 1).astype(jnp.int32)
        inside_offset = row_ids - starts[segment_piece]
        return adapter_update.reshape(ADAPTERS_USED * SEGMENT_ROWS_TOP, VALUE_OUT_WIDTH)[(segment_piece * SEGMENT_ROWS_TOP + inside_offset).astype(jnp.int32)]

    deltas = lax.map(instance_delta, (tokens.reshape(N_STORE, ROWS_DEV, MODEL_WIDTH), requests, segment_row_lengths))
    return (base_values + deltas.reshape(ROWS, VALUE_OUT_WIDTH)).astype(jnp.bfloat16)
```

```python
import functools

import jax
import jax.numpy as jnp
from jax import lax
from jax.sharding import PartitionSpec as P

adapter_alpha = 32.0
CAPACITY_PARTS = (4, 5, 6, 8, 16)


def segment_layout(lengths, segment_capacity, row_count, mixture_count):
    starts = jnp.cumsum(lengths) - lengths
    step_ids = jnp.arange(segment_capacity, dtype=jnp.int32)
    window_index = jnp.minimum(starts[:, None] + step_ids[None, :], row_count - 1)
    row_ids = jnp.arange(row_count, dtype=jnp.int32)
    segment_piece = jnp.sum((starts[None, :] <= row_ids[:, None]).astype(jnp.int32), axis=1) - 1
    is_segment = segment_piece[:, None] == jnp.arange(mixture_count, dtype=jnp.int32)[None, :]
    start_of = jnp.sum(jnp.where(is_segment, starts[None, :], 0), axis=1)
    return (window_index, segment_piece * segment_capacity + (row_ids - start_of))


def column_gain(adapter_rank_list, desired_identifiers, highest_rank):
    table_ids = jnp.arange(adapter_rank_list.shape[0], dtype=jnp.int32)
    chosen_ranks = jnp.sum(
        jnp.where(
            desired_identifiers[:, None] == table_ids[None, :], adapter_rank_list[None, :], 0
        ),
        axis=1,
    )
    column_ids = jnp.arange(highest_rank, dtype=jnp.int32)
    retained_columns = (column_ids[None, :] < chosen_ranks[:, None]).astype(jnp.float32)
    return retained_columns * (adapter_alpha / chosen_ranks.astype(jnp.float32))[:, None]


def local(
    tokens,
    value_matrix,
    adapter_down_matrix,
    adapter_up_matrix,
    adapter_rank_list,
    requests,
    segment_row_lengths,
):
    row_count = tokens.shape[0]
    adapter_tally = adapter_down_matrix.shape[0]
    highest_rank = adapter_down_matrix.shape[2]
    mixture_count = requests.shape[1]
    segment_capacity = 2 * row_count // max(mixture_count, 4)
    base_part = jnp.dot(tokens, value_matrix, preferred_element_type=jnp.float32)
    base_values = lax.psum_scatter(base_part, "tp", scatter_dimension=1, tiled=True)
    desired_identifiers = requests[0]
    window_index, row_slot = segment_layout(
        segment_row_lengths[0], segment_capacity, row_count, mixture_count
    )
    segment_spans = tokens[window_index]
    owner_of = desired_identifiers // adapter_tally
    every_request = lax.all_gather(requests, "store", axis=0, tiled=True)
    my_owner = lax.axis_index("store")
    is_mine = every_request // adapter_tally == my_owner
    nearby_position = jnp.sum(
        jnp.where(is_mine, every_request - my_owner * adapter_tally, 0), axis=1
    )
    pulled_down, pulled_up = (
        lax.all_to_all(
            adapter_down_matrix[nearby_position], "store", split_axis=0, concat_axis=0, tiled=True
        ),
        lax.all_to_all(
            adapter_up_matrix[nearby_position], "store", split_axis=0, concat_axis=0, tiled=True
        ),
    )
    segment_down = pulled_down[owner_of]
    segment_up = pulled_up[owner_of]
    adapter_middle = jnp.einsum(
        "kng,kgz->knz", segment_spans, segment_down, preferred_element_type=jnp.float32
    )
    adapter_middle = lax.psum(adapter_middle, "tp")
    column_factors = column_gain(adapter_rank_list, desired_identifiers, highest_rank)
    scaled_update = (adapter_middle * column_factors[:, None, :]).astype(jnp.bfloat16)
    adapter_update = jnp.einsum(
        "poa,pal->pol", scaled_update, segment_up, preferred_element_type=jnp.float32
    )
    flattened_delta = adapter_update.reshape(
        mixture_count * segment_capacity, adapter_update.shape[2]
    )
    return (base_values + flattened_delta[row_slot]).astype(jnp.bfloat16)

def exclusive_sum(lens):
    return jnp.cumsum(lens, axis=-1) - lens


def one_hot_rows(height, source):
    q = lax.broadcasted_iota(jnp.int32, (height, source.shape[0]), 0)
    return (q == source[None, :]).astype(jnp.bfloat16)


def copy_columns(values, chosen):
    return jnp.dot(values, chosen, preferred_element_type=jnp.float32)


def exchange_sum(x, n_tp):
    if n_tp != 2:
        return lax.psum(x, "tp")
    return x + lax.ppermute(x, "tp", [(0, 1), (1, 0)])


def link_tables(asked, ranks, n_chips, owner_chip):
    dest = jnp.arange(n_chips, dtype=jnp.int32)
    right, left = [], []
    for z in range(n_chips):
        beyond = jnp.any(asked & (dest > z)[:, None], axis=0) & (owner_chip <= z)
        right.append(jnp.where(beyond, ranks, 0))
        before = jnp.any(asked & (dest < z)[:, None], axis=0) & (owner_chip >= z)
        left.append(jnp.where(before, ranks, 0))
    return jnp.stack(right), jnp.stack(left)


def hop_plan(
    capacity,
    n_store,
    n_tp,
    tokens,
    value_matrix,
    down,
    up,
    ranks,
    all_requests,
    lengths,
    right_lens,
    left_lens,
):
    rows, feats = tokens.shape
    per_dev, _, rank_cap = down.shape
    outs = up.shape[2]
    n_seg = all_requests.shape[1]
    n_chips = n_store // 2
    own_width = 2 * per_dev * rank_cap
    half = feats // 2 + outs // 2
    depth = next(d for d in (384, 256, 128, 64, 32, 16, half) if half % d == 0)
    chunks = half // depth
    store = lax.axis_index("store")
    z, core = store // 2, lax.rem(store, 2)
    swap = [(i, i ^ 1) for i in range(n_store)]
    rightward = [(i, i + 2) for i in range(n_store - 2)]
    leftward = [(i + 2, i) for i in range(n_store - 2)]

    down_rows = down.transpose(1, 0, 2).reshape(2, feats // 2, per_dev * rank_cap)
    up_rows = up.transpose(2, 0, 1).reshape(2, outs // 2, per_dev * rank_cap)
    both = jnp.concatenate([down_rows, up_rows], axis=1)
    mine = lax.dynamic_index_in_dim(both, core, 0, keepdims=False)
    given = lax.dynamic_index_in_dim(both, 1 - core, 0, keepdims=False)
    got = lax.ppermute(given, "store", swap)
    first = core == 0
    own = jnp.concatenate([jnp.where(first, mine, got), jnp.where(first, got, mine)], axis=1)

    ids = jnp.arange(ranks.shape[0], dtype=jnp.int32)
    owner_chip = ids // (2 * per_dev)
    own_at = (ids - z * 2 * per_dev) * rank_cap
    is_own = owner_chip == z
    right_at, left_at = exclusive_sum(right_lens), exclusive_sum(left_lens)

    def row_of(table, at):
        return lax.dynamic_index_in_dim(table, jnp.clip(at, 0, n_chips - 1), 0, keepdims=False)

    in_right_at, in_left_at = row_of(right_at, z - 1), row_of(left_at, z + 1)
    spots = jnp.arange(capacity, dtype=jnp.int32)

    def forward(lens, out_at, in_at):
        active = (out_at[:, None] <= spots) & (spots < (out_at + lens)[:, None])
        offset = spots[None, :] - out_at[:, None]

        def source(kept, base):
            taken = active & kept[:, None]
            return jnp.sum(jnp.where(taken, offset + base[:, None] + 1, 0), axis=0) - 1

        return (
            one_hot_rows(own_width, source(is_own, own_at)),
            one_hot_rows(capacity, source(~is_own, in_at)),
        )

    own_r, pass_r = forward(row_of(right_lens, z), row_of(right_at, z), in_right_at)
    own_l, pass_l = forward(row_of(left_lens, z), row_of(left_at, z), in_left_at)

    columns = jnp.arange(rank_cap, dtype=jnp.int32)

    def extract(instance):
        wanted = lax.dynamic_index_in_dim(all_requests, instance, 0, keepdims=False)
        is_it = wanted[:, None] == ids[None, :]

        def source(kept, base):
            at = jnp.sum(jnp.where(is_it & kept[None, :], base[None, :] + 1, 0), axis=1) - 1
            size = jnp.sum(jnp.where(is_it & kept[None, :], ranks[None, :], 0), axis=1)
            spot = jnp.where(columns[None, :] < size[:, None], at[:, None] + columns[None, :], -1)
            return spot.reshape(n_seg * rank_cap)

        return (
            source(is_own, own_at),
            source(owner_chip < z, in_right_at),
            source(owner_chip > z, in_left_at),
        )

    sib, my = extract(z * 2 + 1 - core), extract(store)
    take_own, take_r, take_l = (
        one_hot_rows(height, jnp.concatenate([sib[i], my[i]]))
        for i, height in enumerate((own_width, capacity, capacity))
    )
    start_r = copy_columns(own, own_r).astype(jnp.bfloat16)
    start_l = copy_columns(own, own_l).astype(jnp.bfloat16)

    steps = chunks + n_chips - 2
    in_r = in_l = None
    parts_r, parts_l = [], []
    for t in range(steps):
        at_r = jnp.clip(t - z, 0, chunks - 1) * depth
        at_l = jnp.clip(t - (n_chips - 1 - z), 0, chunks - 1) * depth
        send_r = lax.dynamic_slice_in_dim(start_r, at_r, depth, 0)
        send_l = lax.dynamic_slice_in_dim(start_l, at_l, depth, 0)
        if t > 0:
            send_r = (send_r + copy_columns(in_r, pass_r)).astype(jnp.bfloat16)
            send_l = (send_l + copy_columns(in_l, pass_l)).astype(jnp.bfloat16)
        in_r = lax.ppermute(send_r, "store", rightward)
        in_l = lax.ppermute(send_l, "store", leftward)
        parts_r.append(copy_columns(in_r, take_r).astype(jnp.bfloat16))
        parts_l.append(copy_columns(in_l, take_l).astype(jnp.bfloat16))
    base = jnp.dot(tokens, value_matrix, preferred_element_type=jnp.float32)
    if n_tp == 2:
        tp = lax.axis_index("tp")
        far = lax.dynamic_slice_in_dim(base, (1 - tp) * outs, outs, 1)
        near = lax.dynamic_slice_in_dim(base, tp * outs, outs, 1)
        base_values = near + lax.ppermute(far, "tp", [(0, 1), (1, 0)])
    else:
        base_values = lax.psum_scatter(base, "tp", scatter_dimension=1, tiled=True)
    from_r = lax.dynamic_slice_in_dim(
        jnp.concatenate(parts_r, 0), jnp.clip(z - 1, 0, n_chips - 2) * depth, half, 0
    )
    from_l = lax.dynamic_slice_in_dim(
        jnp.concatenate(parts_l, 0), jnp.clip(n_chips - 2 - z, 0, n_chips - 2) * depth, half, 0
    )
    from_own = copy_columns(own, take_own).astype(jnp.bfloat16)
    found = from_own + jnp.where(z > 0, from_r, 0) + jnp.where(z < n_chips - 1, from_l, 0)
    wide = n_seg * rank_cap
    here = found[:, wide:]
    there = lax.ppermute(found[:, :wide], "store", swap)
    low, high = jnp.where(first, here, there), jnp.where(first, there, here)
    cut = feats // 2
    inner = jnp.dot(tokens[:, :cut], low[:cut], preferred_element_type=jnp.float32)
    inner = inner + jnp.dot(tokens[:, cut:], high[:cut], preferred_element_type=jnp.float32)
    starts = exclusive_sum(lengths)
    row_ids = jnp.arange(rows, dtype=jnp.int32)
    inside = (starts[None, :] <= row_ids[:, None]) & (
        row_ids[:, None] < (starts + lengths)[None, :]
    )
    inner = jnp.sum(jnp.where(inside[:, :, None], inner.reshape(rows, n_seg, rank_cap), 0.0), axis=1)
    inner = exchange_sum(inner, n_tp)
    my_request = lax.dynamic_index_in_dim(all_requests, store, 0, keepdims=False)
    factors = column_gain(ranks, my_request, rank_cap)
    scaled = (inner[:, None, :] * factors[None, :, :]).astype(jnp.bfloat16)
    scaled = jnp.where(inside[:, :, None], scaled, 0).reshape(rows, wide)
    up_all = jnp.concatenate([low[cut:], high[cut:]], axis=0)
    delta = lax.dot_general(
        scaled, up_all, (((1,), (1,)), ((), ())), preferred_element_type=jnp.float32
    )
    return (base_values + delta).astype(jnp.bfloat16)


def by_hops(n_grp, n_store, n_tp, tokens, value_matrix, down, up, rank_list, requests, lengths):
    n_chips, per_dev, rank_cap = n_store // 2, down.shape[0], down.shape[2]
    n_seg = requests.shape[1]
    n_adapters = n_store * per_dev
    store, grp = lax.axis_index("store"), lax.axis_index("grp")
    my_ranks = lax.dynamic_slice_in_dim(rank_list, store * per_dev, per_dev, 0)
    note = jnp.concatenate([requests[0], my_ranks])[None, :]
    notes = lax.all_gather(note, ("grp", "store"), axis=0, tiled=True)
    notes = notes.reshape(n_grp, n_store, n_seg + per_dev)
    ids = jnp.arange(n_adapters, dtype=jnp.int32)
    owner_chip = ids // (2 * per_dev)
    tables, load = [], 0
    for g in range(n_grp):
        asked = notes[g, :, :n_seg].reshape(n_chips, 2 * n_seg)
        asked = jnp.any(asked[:, :, None] == ids[None, None, :], axis=1)
        ranks = notes[g, :, n_seg:].reshape(n_adapters)
        right, left = link_tables(asked, ranks, n_chips, owner_chip)
        tables.append(jnp.stack([right, left]))
        load = jnp.maximum(load, jnp.max(jnp.sum(tables[-1], axis=-1)))
    mine = lax.dynamic_index_in_dim(jnp.stack(tables), grp, 0, keepdims=False)
    all_requests = lax.dynamic_index_in_dim(notes[:, :, :n_seg], grp, 0, keepdims=False)
    most = n_chips * per_dev * rank_cap
    sizes = [most * part // 16 for part in CAPACITY_PARTS]
    branches = [
        lambda *ops, size=size: hop_plan(size, n_store, n_tp, *ops) for size in sizes
    ]
    branch = sum((load > size).astype(jnp.int32) for size in sizes[:-1])
    return lax.switch(
        branch, branches, tokens, value_matrix, down, up, rank_list, all_requests,
        lengths[0], mine[0], mine[1],
    )


def solution(mesh):
    in_specs = (
        P(("grp", "store"), "tp"),
        P("tp", None),
        P(("grp", "store"), "tp", None),
        P(("grp", "store"), None, "tp"),
        P("grp"),
        P(("grp", "store"), None),
        P(("grp", "store"), None),
    )
    out_specs = P(("grp", "store"), "tp")
    n_grp, n_store, n_tp = (mesh.shape[axis] for axis in ("grp", "store", "tp"))
    body = local
    if n_store % 2 == 0 and 4 <= n_store <= 8:
        body = functools.partial(by_hops, n_grp, n_store, n_tp)
    return jax.shard_map(body, mesh=mesh, in_specs=in_specs, out_specs=out_specs, check_vma=False)
```

```python
import functools

import jax
import jax.numpy as jnp
from jax import lax
from jax.experimental import pallas as pl
from jax.experimental.pallas import tpu as pltpu
from jax.sharding import PartitionSpec as P

adapter_alpha = 32.0
CAPACITY_PARTS = (5, 6, 8, 16)
KERNEL = True


def segment_layout(lengths, segment_capacity, row_count, mixture_count):
    starts = jnp.cumsum(lengths) - lengths
    step_ids = jnp.arange(segment_capacity, dtype=jnp.int32)
    window_index = jnp.minimum(starts[:, None] + step_ids[None, :], row_count - 1)
    row_ids = jnp.arange(row_count, dtype=jnp.int32)
    segment_piece = jnp.sum((starts[None, :] <= row_ids[:, None]).astype(jnp.int32), axis=1) - 1
    is_segment = segment_piece[:, None] == jnp.arange(mixture_count, dtype=jnp.int32)[None, :]
    start_of = jnp.sum(jnp.where(is_segment, starts[None, :], 0), axis=1)
    return (window_index, segment_piece * segment_capacity + (row_ids - start_of))


def column_gain(adapter_rank_list, desired_identifiers, highest_rank):
    table_ids = jnp.arange(adapter_rank_list.shape[0], dtype=jnp.int32)
    chosen_ranks = jnp.sum(
        jnp.where(
            desired_identifiers[:, None] == table_ids[None, :], adapter_rank_list[None, :], 0
        ),
        axis=1,
    )
    column_ids = jnp.arange(highest_rank, dtype=jnp.int32)
    retained_columns = (column_ids[None, :] < chosen_ranks[:, None]).astype(jnp.float32)
    return retained_columns * (adapter_alpha / chosen_ranks.astype(jnp.float32))[:, None]


def local(
    tokens,
    value_matrix,
    adapter_down_matrix,
    adapter_up_matrix,
    adapter_rank_list,
    requests,
    segment_row_lengths,
):
    row_count = tokens.shape[0]
    adapter_tally = adapter_down_matrix.shape[0]
    highest_rank = adapter_down_matrix.shape[2]
    mixture_count = requests.shape[1]
    segment_capacity = 2 * row_count // max(mixture_count, 4)
    base_part = jnp.dot(tokens, value_matrix, preferred_element_type=jnp.float32)
    base_values = lax.psum_scatter(base_part, "tp", scatter_dimension=1, tiled=True)
    desired_identifiers = requests[0]
    window_index, row_slot = segment_layout(
        segment_row_lengths[0], segment_capacity, row_count, mixture_count
    )
    segment_spans = tokens[window_index]
    owner_of = desired_identifiers // adapter_tally
    every_request = lax.all_gather(requests, "store", axis=0, tiled=True)
    my_owner = lax.axis_index("store")
    is_mine = every_request // adapter_tally == my_owner
    nearby_position = jnp.sum(
        jnp.where(is_mine, every_request - my_owner * adapter_tally, 0), axis=1
    )
    pulled_down, pulled_up = (
        lax.all_to_all(
            adapter_down_matrix[nearby_position], "store", split_axis=0, concat_axis=0, tiled=True
        ),
        lax.all_to_all(
            adapter_up_matrix[nearby_position], "store", split_axis=0, concat_axis=0, tiled=True
        ),
    )
    segment_down = pulled_down[owner_of]
    segment_up = pulled_up[owner_of]
    adapter_middle = jnp.einsum(
        "kng,kgz->knz", segment_spans, segment_down, preferred_element_type=jnp.float32
    )
    adapter_middle = lax.psum(adapter_middle, "tp")
    column_factors = column_gain(adapter_rank_list, desired_identifiers, highest_rank)
    scaled_update = (adapter_middle * column_factors[:, None, :]).astype(jnp.bfloat16)
    adapter_update = jnp.einsum(
        "poa,pal->pol", scaled_update, segment_up, preferred_element_type=jnp.float32
    )
    flattened_delta = adapter_update.reshape(
        mixture_count * segment_capacity, adapter_update.shape[2]
    )
    return (base_values + flattened_delta[row_slot]).astype(jnp.bfloat16)

def exclusive_sum(lens):
    return jnp.cumsum(lens, axis=-1) - lens


def one_hot_rows(height, source):
    q = lax.broadcasted_iota(jnp.int32, (height, source.shape[0]), 0)
    return (q == source[None, :]).astype(jnp.bfloat16)


def copy_columns(values, chosen):
    return jnp.dot(values, chosen, preferred_element_type=jnp.float32)


def exchange_sum(x, n_tp):
    if n_tp != 2:
        return lax.psum(x, "tp")
    return x + lax.ppermute(x, "tp", [(0, 1), (1, 0)])


def link_tables(asked, ranks, n_chips, owner_chip):
    dest = jnp.arange(n_chips, dtype=jnp.int32)
    right, left = [], []
    for z in range(n_chips):
        beyond = jnp.any(asked & (dest > z)[:, None], axis=0) & (owner_chip <= z)
        right.append(jnp.where(beyond, ranks, 0))
        before = jnp.any(asked & (dest < z)[:, None], axis=0) & (owner_chip >= z)
        left.append(jnp.where(before, ranks, 0))
    return jnp.stack(right), jnp.stack(left)


def hop_plan(
    capacity,
    n_store,
    n_tp,
    identity,
    rank_cap,
    outs,
    tokens,
    far,
    near,
    own,
    ranks,
    all_requests,
    lengths,
    right_lens,
    left_lens,
):
    rows, feats = tokens.shape
    per_dev = own.shape[1] // (2 * rank_cap)
    n_seg = all_requests.shape[1]
    n_chips = n_store // 2
    own_width = 2 * per_dev * rank_cap
    half = feats // 2 + outs // 2
    depth = next(d for d in (384, 256, 128, 64, 32, 16, half) if half % d == 0)
    chunks = half // depth
    store = lax.axis_index("store")
    z, core = store // 2, lax.rem(store, 2)
    swap = [(i, i ^ 1) for i in range(n_store)]
    rightward = [(i, i + 2) for i in range(n_store - 2)]
    leftward = [(i + 2, i) for i in range(n_store - 2)]

    ids = jnp.arange(ranks.shape[0], dtype=jnp.int32)
    owner_chip = ids // (2 * per_dev)
    in_turn = jnp.where(ids // per_dev == store, 0, per_dev) + lax.rem(ids, per_dev)
    own_at = in_turn * rank_cap
    is_own = owner_chip == z
    right_at, left_at = exclusive_sum(right_lens), exclusive_sum(left_lens)

    def row_of(table, at):
        return lax.dynamic_index_in_dim(table, jnp.clip(at, 0, n_chips - 1), 0, keepdims=False)

    in_right_at, in_left_at = row_of(right_at, z - 1), row_of(left_at, z + 1)
    spots = jnp.arange(capacity, dtype=jnp.int32)

    def forward(lens, out_at, in_at):
        active = (out_at[:, None] <= spots) & (spots < (out_at + lens)[:, None])
        offset = spots[None, :] - out_at[:, None]

        def source(kept, base):
            taken = active & kept[:, None]
            return jnp.sum(jnp.where(taken, offset + base[:, None] + 1, 0), axis=0) - 1

        return (
            one_hot_rows(own_width, source(is_own, own_at)),
            one_hot_rows(capacity, source(~is_own, in_at)),
        )

    own_r, pass_r = forward(row_of(right_lens, z), row_of(right_at, z), in_right_at)
    own_l, pass_l = forward(row_of(left_lens, z), row_of(left_at, z), in_left_at)

    columns = jnp.arange(rank_cap, dtype=jnp.int32)

    def extract(instance):
        wanted = lax.dynamic_index_in_dim(all_requests, instance, 0, keepdims=False)
        is_it = wanted[:, None] == ids[None, :]

        def source(kept, base):
            at = jnp.sum(jnp.where(is_it & kept[None, :], base[None, :] + 1, 0), axis=1) - 1
            size = jnp.sum(jnp.where(is_it & kept[None, :], ranks[None, :], 0), axis=1)
            spot = jnp.where(columns[None, :] < size[:, None], at[:, None] + columns[None, :], -1)
            return spot.reshape(n_seg * rank_cap)

        return (
            source(is_own, own_at),
            source(owner_chip < z, in_right_at),
            source(owner_chip > z, in_left_at),
        )

    sib, my = extract(z * 2 + 1 - core), extract(store)
    take_own, take_r, take_l = (
        one_hot_rows(height, jnp.concatenate([sib[i], my[i]]))
        for i, height in enumerate((own_width, capacity, capacity))
    )
    start_r = copy_columns(own, own_r).astype(jnp.bfloat16)
    start_l = copy_columns(own, own_l).astype(jnp.bfloat16)
    base_values = near + lax.ppermute(far, "tp", [(0, 1), (1, 0)])
    if identity is not None:
        found = hop_call(
            identity, n_chips, own, start_r, start_l, pass_r, pass_l, take_own, take_r, take_l
        )
    else:
        steps = chunks + n_chips - 2
        in_r = in_l = None
        parts_r, parts_l = [], []
        for t in range(steps):
            at_r = jnp.clip(t - z, 0, chunks - 1) * depth
            at_l = jnp.clip(t - (n_chips - 1 - z), 0, chunks - 1) * depth
            send_r = lax.dynamic_slice_in_dim(start_r, at_r, depth, 0)
            send_l = lax.dynamic_slice_in_dim(start_l, at_l, depth, 0)
            if t > 0:
                send_r = (send_r + copy_columns(in_r, pass_r)).astype(jnp.bfloat16)
                send_l = (send_l + copy_columns(in_l, pass_l)).astype(jnp.bfloat16)
            in_r = lax.ppermute(send_r, "store", rightward)
            in_l = lax.ppermute(send_l, "store", leftward)
            if t == 3:
                in_r, base_values = lax.optimization_barrier((in_r, base_values))
            parts_r.append(copy_columns(in_r, take_r).astype(jnp.bfloat16))
            parts_l.append(copy_columns(in_l, take_l).astype(jnp.bfloat16))
        from_r = lax.dynamic_slice_in_dim(
            jnp.concatenate(parts_r, 0), jnp.clip(z - 1, 0, n_chips - 2) * depth, half, 0
        )
        from_l = lax.dynamic_slice_in_dim(
            jnp.concatenate(parts_l, 0), jnp.clip(n_chips - 2 - z, 0, n_chips - 2) * depth, half, 0
        )
        from_own = copy_columns(own, take_own).astype(jnp.bfloat16)
        found = from_own + jnp.where(z > 0, from_r, 0) + jnp.where(z < n_chips - 1, from_l, 0)
    wide, first = n_seg * rank_cap, core == 0
    here = found[:, wide:]
    there = lax.ppermute(found[:, :wide], "store", swap)
    low, high = jnp.where(first, here, there), jnp.where(first, there, here)
    cut = feats // 2
    inner = jnp.dot(tokens[:, :cut], low[:cut], preferred_element_type=jnp.float32)
    inner = inner + jnp.dot(tokens[:, cut:], high[:cut], preferred_element_type=jnp.float32)
    starts = exclusive_sum(lengths)
    row_ids = jnp.arange(rows, dtype=jnp.int32)
    inside = (starts[None, :] <= row_ids[:, None]) & (
        row_ids[:, None] < (starts + lengths)[None, :]
    )
    inner = jnp.sum(jnp.where(inside[:, :, None], inner.reshape(rows, n_seg, rank_cap), 0.0), axis=1)
    inner = exchange_sum(inner, n_tp)
    my_request = lax.dynamic_index_in_dim(all_requests, store, 0, keepdims=False)
    factors = column_gain(ranks, my_request, rank_cap)
    scaled = (inner[:, None, :] * factors[None, :, :]).astype(jnp.bfloat16)
    scaled = jnp.where(inside[:, :, None], scaled, 0).reshape(rows, wide)
    up_all = jnp.concatenate([low[cut:], high[cut:]], axis=0)
    delta = lax.dot_general(
        scaled, up_all, (((1,), (1,)), ((), ())), preferred_element_type=jnp.float32
    )
    return (base_values + delta).astype(jnp.bfloat16)


def share(x, axis, count):
    place, width = lax.axis_index(axis), 1
    while width < count:
        other = lax.ppermute(x, axis, [(i, i ^ width) for i in range(count)])
        low = (place // width) % 2 == 0
        x = jnp.concatenate([jnp.where(low, x, other), jnp.where(low, other, x)], axis=0)
        width *= 2
    return x


def before_hops(n_store, tokens, value_matrix, down, up):
    feats, outs, per_dev = tokens.shape[1], up.shape[2], down.shape[0]
    tp, core = lax.axis_index("tp"), lax.rem(lax.axis_index("store"), 2)
    cut_d, cut_u = feats // 2, outs // 2
    swap = [(i, i ^ 1) for i in range(n_store)]

    def halves(which):
        return (
            lax.dynamic_slice_in_dim(down, which * cut_d, cut_d, 1),
            lax.dynamic_slice_in_dim(up, which * cut_u, cut_u, 2),
        )

    got_d, got_u = (lax.ppermute(x, "store", swap) for x in halves(1 - core))
    mine_d, mine_u = halves(core)
    down_rows = jnp.concatenate([x[a] for x in (mine_d, got_d) for a in range(per_dev)], axis=1)
    up_rows = jnp.concatenate([x[a].T for x in (mine_u, got_u) for a in range(per_dev)], axis=1)
    own = jnp.concatenate([down_rows, up_rows], axis=0)
    far = lax.dynamic_slice_in_dim(value_matrix, (1 - tp) * outs, outs, 1)
    near = lax.dynamic_slice_in_dim(value_matrix, tp * outs, outs, 1)
    return copy_columns(tokens, far), copy_columns(tokens, near), own


def hop_kernel(
    n_chips, depth, own, start_r, start_l, pass_r, pass_l, take_own, take_r, take_l,
    found, out_r, out_l, in_r, in_l, sent_r, sent_l, came_r, came_l,
):
    store = lax.axis_index("store")
    z = store // 2
    chunks = own.shape[0] // depth
    right, left = z < n_chips - 1, z > 0
    barrier = pltpu.get_barrier_semaphore()

    @pl.when(right)
    def _():
        pl.semaphore_signal(
            barrier, inc=1, device_id={"store": store + 2}, device_id_type=pl.DeviceIdType.MESH
        )

    @pl.when(left)
    def _():
        pl.semaphore_signal(
            barrier, inc=1, device_id={"store": store - 2}, device_id_type=pl.DeviceIdType.MESH
        )

    pl.semaphore_wait(barrier, right.astype(jnp.int32) + left.astype(jnp.int32))

    streams = (
        (z, right, left, store + 2, start_r, pass_r, take_r, out_r, in_r, sent_r, came_r),
        (
            n_chips - 1 - z, left, right, store - 2,
            start_l, pass_l, take_l, out_l, in_l, sent_l, came_l,
        ),
    )

    def copy(stream, k):
        _, _, _, to, _, _, _, out, into, sent, came = stream
        rows = pl.ds(pl.multiple_of(k * depth, depth), depth)
        return pltpu.make_async_remote_copy(
            src_ref=out.at[rows, :],
            dst_ref=into.at[rows, :],
            send_sem=sent.at[k],
            recv_sem=came.at[k],
            device_id={"store": to},
            device_id_type=pl.DeviceIdType.MESH,
        )

    def step(t, carry):
        for stream in streams:
            order, gives, gets, _, start, onward, _, out, into, _, _ = stream
            k = t - 2 * order
            live = (k >= 0) & (k < chunks)

            @pl.when(live & gets)
            def _(stream=stream, k=k):
                copy(stream, k).wait_recv()

            @pl.when(live & gives & gets)
            def _(k=k, start=start, onward=onward, out=out, into=into):
                rows = pl.ds(pl.multiple_of(k * depth, depth), depth)
                moved = copy_columns(into[rows, :], onward[...])
                out[rows, :] = start[rows, :] + moved.astype(jnp.bfloat16)

            @pl.when(live & gives & jnp.logical_not(gets))
            def _(k=k, start=start, out=out):
                rows = pl.ds(pl.multiple_of(k * depth, depth), depth)
                out[rows, :] = start[rows, :]

            @pl.when(live & gives)
            def _(stream=stream, k=k):
                copy(stream, k).start()

        @pl.when(t < chunks)
        def _():
            rows = pl.ds(pl.multiple_of(t * depth, depth), depth)
            found[rows, :] = copy_columns(own[rows, :], take_own[...]).astype(jnp.bfloat16)

        for stream in streams:
            order, _, gets, _, _, _, take, _, into, _, _ = stream
            k = t - 2 * order

            @pl.when((k >= 0) & (k < chunks) & gets)
            def _(k=k, take=take, into=into):
                rows = pl.ds(pl.multiple_of(k * depth, depth), depth)
                picked = copy_columns(into[rows, :], take[...]).astype(jnp.bfloat16)
                found[rows, :] = found[rows, :] + picked

        return carry

    lax.fori_loop(0, chunks + 2 * (n_chips - 1), step, 0)

    def finish(k, carry):
        for stream in streams:

            @pl.when(stream[1])
            def _(stream=stream):
                copy(stream, k).wait_send()

        return carry

    lax.fori_loop(0, chunks, finish, 0)


def hop_call(identity, n_chips, own, start_r, start_l, pass_r, pass_l, take_own, take_r, take_l):
    half, capacity = start_r.shape
    depth = 128 if half % 128 == 0 else 16
    line = pltpu.VMEM((half, capacity), jnp.bfloat16)
    marks = pltpu.SemaphoreType.DMA((half // depth,))
    return pl.pallas_call(
        functools.partial(hop_kernel, n_chips, depth),
        out_shape=jax.ShapeDtypeStruct((half, take_own.shape[1]), jnp.bfloat16),
        in_specs=[pl.BlockSpec(memory_space=pltpu.VMEM)] * 8,
        out_specs=pl.BlockSpec(memory_space=pltpu.VMEM),
        scratch_shapes=[line] * 4 + [marks] * 4,
        compiler_params=pltpu.CompilerParams(
            collective_id=identity, has_side_effects=True, vmem_limit_bytes=56 * 1024 * 1024
        ),
    )(own, start_r, start_l, pass_r, pass_l, take_own, take_r, take_l)


def by_hops(n_grp, n_store, n_tp, tokens, value_matrix, down, up, rank_list, requests, lengths):
    n_chips, per_dev, rank_cap = n_store // 2, down.shape[0], down.shape[2]
    n_seg = requests.shape[1]
    n_adapters = n_store * per_dev
    store, grp = lax.axis_index("store"), lax.axis_index("grp")
    my_ranks = lax.dynamic_slice_in_dim(rank_list, store * per_dev, per_dev, 0)
    note = jnp.concatenate([requests[0], my_ranks])[None, :]
    notes = share(share(note, "store", n_store), "grp", n_grp)
    notes = notes.reshape(n_grp, n_store, n_seg + per_dev)
    ids = jnp.arange(n_adapters, dtype=jnp.int32)
    owner_chip = ids // (2 * per_dev)
    tables, load = [], 0
    for g in range(n_grp):
        asked = notes[g, :, :n_seg].reshape(n_chips, 2 * n_seg)
        asked = jnp.any(asked[:, :, None] == ids[None, None, :], axis=1)
        ranks = notes[g, :, n_seg:].reshape(n_adapters)
        right, left = link_tables(asked, ranks, n_chips, owner_chip)
        tables.append(jnp.stack([right, left]))
        load = jnp.maximum(load, jnp.max(jnp.sum(tables[-1], axis=-1)))
    mine = lax.dynamic_index_in_dim(jnp.stack(tables), grp, 0, keepdims=False)
    all_requests = lax.dynamic_index_in_dim(notes[:, :, :n_seg], grp, 0, keepdims=False)
    far, near, own = before_hops(n_store, tokens, value_matrix, down, up)
    most = n_chips * per_dev * rank_cap
    sizes = [most * part // 16 for part in CAPACITY_PARTS]
    branches = [
        functools.partial(
            hop_plan, size, n_store, n_tp, i if KERNEL and i + 1 < len(sizes) else None,
            rank_cap, up.shape[2],
        )
        for i, size in enumerate(sizes)
    ]
    branch = sum((load > size).astype(jnp.int32) for size in sizes[:-1])
    return lax.switch(
        branch, branches, tokens, far, near, own, rank_list, all_requests,
        lengths[0], mine[0], mine[1],
    )


def solution(mesh):
    in_specs = (
        P(("grp", "store"), "tp"),
        P("tp", None),
        P(("grp", "store"), "tp", None),
        P(("grp", "store"), None, "tp"),
        P("grp"),
        P(("grp", "store"), None),
        P(("grp", "store"), None),
    )
    out_specs = P(("grp", "store"), "tp")
    n_grp, n_store, n_tp = (mesh.shape[axis] for axis in ("grp", "store", "tp"))
    body = local
    if n_store % 2 == 0 and n_tp == 2 and n_store in (4, 8) and n_grp in (1, 2):
        body = functools.partial(by_hops, n_grp, n_store, n_tp)
    return jax.shard_map(body, mesh=mesh, in_specs=in_specs, out_specs=out_specs, check_vma=False)
```

```python
import functools

import jax
import jax.numpy as jnp
from jax import lax
from jax.experimental import pallas as pl
from jax.experimental.pallas import tpu as pltpu
from jax.sharding import PartitionSpec as P

adapter_alpha = 32.0
CAPACITY_PARTS = (5, 6, 7, 16)
KERNEL = True


def segment_layout(lengths, segment_capacity, row_count, mixture_count):
    starts = jnp.cumsum(lengths) - lengths
    step_ids = jnp.arange(segment_capacity, dtype=jnp.int32)
    window_index = jnp.minimum(starts[:, None] + step_ids[None, :], row_count - 1)
    row_ids = jnp.arange(row_count, dtype=jnp.int32)
    segment_piece = jnp.sum((starts[None, :] <= row_ids[:, None]).astype(jnp.int32), axis=1) - 1
    is_segment = segment_piece[:, None] == jnp.arange(mixture_count, dtype=jnp.int32)[None, :]
    start_of = jnp.sum(jnp.where(is_segment, starts[None, :], 0), axis=1)
    return (window_index, segment_piece * segment_capacity + (row_ids - start_of))


def column_gain(adapter_rank_list, desired_identifiers, highest_rank):
    table_ids = jnp.arange(adapter_rank_list.shape[0], dtype=jnp.int32)
    chosen_ranks = jnp.sum(
        jnp.where(
            desired_identifiers[:, None] == table_ids[None, :], adapter_rank_list[None, :], 0
        ),
        axis=1,
    )
    column_ids = jnp.arange(highest_rank, dtype=jnp.int32)
    retained_columns = (column_ids[None, :] < chosen_ranks[:, None]).astype(jnp.float32)
    return retained_columns * (adapter_alpha / chosen_ranks.astype(jnp.float32))[:, None]


def local(
    tokens,
    value_matrix,
    adapter_down_matrix,
    adapter_up_matrix,
    adapter_rank_list,
    requests,
    segment_row_lengths,
):
    row_count = tokens.shape[0]
    adapter_tally = adapter_down_matrix.shape[0]
    highest_rank = adapter_down_matrix.shape[2]
    mixture_count = requests.shape[1]
    segment_capacity = 2 * row_count // max(mixture_count, 4)
    base_part = jnp.dot(tokens, value_matrix, preferred_element_type=jnp.float32)
    base_values = lax.psum_scatter(base_part, "tp", scatter_dimension=1, tiled=True)
    desired_identifiers = requests[0]
    window_index, row_slot = segment_layout(
        segment_row_lengths[0], segment_capacity, row_count, mixture_count
    )
    segment_spans = tokens[window_index]
    owner_of = desired_identifiers // adapter_tally
    every_request = lax.all_gather(requests, "store", axis=0, tiled=True)
    my_owner = lax.axis_index("store")
    is_mine = every_request // adapter_tally == my_owner
    nearby_position = jnp.sum(
        jnp.where(is_mine, every_request - my_owner * adapter_tally, 0), axis=1
    )
    pulled_down, pulled_up = (
        lax.all_to_all(
            adapter_down_matrix[nearby_position], "store", split_axis=0, concat_axis=0, tiled=True
        ),
        lax.all_to_all(
            adapter_up_matrix[nearby_position], "store", split_axis=0, concat_axis=0, tiled=True
        ),
    )
    segment_down = pulled_down[owner_of]
    segment_up = pulled_up[owner_of]
    adapter_middle = jnp.einsum(
        "kng,kgz->knz", segment_spans, segment_down, preferred_element_type=jnp.float32
    )
    adapter_middle = lax.psum(adapter_middle, "tp")
    column_factors = column_gain(adapter_rank_list, desired_identifiers, highest_rank)
    scaled_update = (adapter_middle * column_factors[:, None, :]).astype(jnp.bfloat16)
    adapter_update = jnp.einsum(
        "poa,pal->pol", scaled_update, segment_up, preferred_element_type=jnp.float32
    )
    flattened_delta = adapter_update.reshape(
        mixture_count * segment_capacity, adapter_update.shape[2]
    )
    return (base_values + flattened_delta[row_slot]).astype(jnp.bfloat16)

def exclusive_sum(lens):
    return jnp.cumsum(lens, axis=-1) - lens


def one_hot_rows(height, source):
    q = lax.broadcasted_iota(jnp.int32, (height, source.shape[0]), 0)
    return (q == source[None, :]).astype(jnp.bfloat16)


def copy_columns(values, chosen):
    return jnp.dot(values, chosen, preferred_element_type=jnp.float32)


def exchange_sum(x, n_tp):
    if n_tp != 2:
        return lax.psum(x, "tp")
    return x + lax.ppermute(x, "tp", [(0, 1), (1, 0)])


def link_tables(asked, ranks, n_chips, owner_chip):
    dest = jnp.arange(n_chips, dtype=jnp.int32)
    right, left = [], []
    for z in range(n_chips):
        beyond = jnp.any(asked & (dest > z)[:, None], axis=0) & (owner_chip <= z)
        right.append(jnp.where(beyond, ranks, 0))
        before = jnp.any(asked & (dest < z)[:, None], axis=0) & (owner_chip >= z)
        left.append(jnp.where(before, ranks, 0))
    return jnp.stack(right), jnp.stack(left)


def hop_plan(
    capacity,
    n_store,
    n_tp,
    identity,
    rank_cap,
    outs,
    tokens,
    value_matrix,
    mine_d,
    got_d,
    up_rows,
    ranks,
    all_requests,
    lengths,
    right_lens,
    left_lens,
):
    rows, feats = tokens.shape
    per_dev = mine_d.shape[0]
    n_seg = all_requests.shape[1]
    n_chips = n_store // 2
    own_width = 2 * per_dev * rank_cap
    half = feats // 2 + outs // 2
    depth = next(d for d in (384, 256, 128, 64, 32, 16, half) if half % d == 0)
    chunks = half // depth
    store = lax.axis_index("store")
    z, core = store // 2, lax.rem(store, 2)
    swap = [(i, i ^ 1) for i in range(n_store)]
    rightward = [(i, i + 2) for i in range(n_store - 2)]
    leftward = [(i + 2, i) for i in range(n_store - 2)]

    ids = jnp.arange(ranks.shape[0], dtype=jnp.int32)
    owner_chip = ids // (2 * per_dev)
    in_turn = jnp.where(ids // per_dev == store, 0, per_dev) + lax.rem(ids, per_dev)
    own_at = in_turn * rank_cap
    is_own = owner_chip == z
    right_at, left_at = exclusive_sum(right_lens), exclusive_sum(left_lens)

    def row_of(table, at):
        return lax.dynamic_index_in_dim(table, jnp.clip(at, 0, n_chips - 1), 0, keepdims=False)

    in_right_at, in_left_at = row_of(right_at, z - 1), row_of(left_at, z + 1)
    spots = jnp.arange(capacity, dtype=jnp.int32)

    def forward(lens, out_at, in_at):
        active = (out_at[:, None] <= spots) & (spots < (out_at + lens)[:, None])
        offset = spots[None, :] - out_at[:, None]

        def source(kept, base):
            taken = active & kept[:, None]
            return jnp.sum(jnp.where(taken, offset + base[:, None] + 1, 0), axis=0) - 1

        return (
            one_hot_rows(own_width, source(is_own, own_at)),
            one_hot_rows(capacity, source(~is_own, in_at)),
        )

    own_r, pass_r = forward(row_of(right_lens, z), row_of(right_at, z), in_right_at)
    own_l, pass_l = forward(row_of(left_lens, z), row_of(left_at, z), in_left_at)

    columns = jnp.arange(rank_cap, dtype=jnp.int32)

    def extract(instance):
        wanted = lax.dynamic_index_in_dim(all_requests, instance, 0, keepdims=False)
        is_it = wanted[:, None] == ids[None, :]

        def source(kept, base):
            at = jnp.sum(jnp.where(is_it & kept[None, :], base[None, :] + 1, 0), axis=1) - 1
            size = jnp.sum(jnp.where(is_it & kept[None, :], ranks[None, :], 0), axis=1)
            spot = jnp.where(columns[None, :] < size[:, None], at[:, None] + columns[None, :], -1)
            return spot.reshape(n_seg * rank_cap)

        return (
            source(is_own, own_at),
            source(owner_chip < z, in_right_at),
            source(owner_chip > z, in_left_at),
        )

    sib, my = extract(z * 2 + 1 - core), extract(store)
    take_own, take_r, take_l = (
        one_hot_rows(height, jnp.concatenate([sib[i], my[i]]))
        for i, height in enumerate((own_width, capacity, capacity))
    )
    wide, first = n_seg * rank_cap, core == 0
    if identity is not None:
        here, there, near, arrived = hop_call(
            identity, n_chips, outs, tokens, value_matrix, mine_d, got_d, up_rows,
            own_r, own_l, pass_r, pass_l, take_own, take_r, take_l,
        )
        base_values = near + arrived
    else:
        own = whole_own(mine_d, got_d, up_rows)
        start_r = copy_columns(own, own_r).astype(jnp.bfloat16)
        start_l = copy_columns(own, own_l).astype(jnp.bfloat16)
        base = copy_columns(tokens, value_matrix)
        tp = lax.axis_index("tp")
        far = lax.dynamic_slice_in_dim(base, (1 - tp) * outs, outs, 1)
        near = lax.dynamic_slice_in_dim(base, tp * outs, outs, 1)
        base_values = near + lax.ppermute(far, "tp", [(0, 1), (1, 0)])
        steps = chunks + n_chips - 2
        in_r = in_l = None
        parts_r, parts_l = [], []
        for t in range(steps):
            at_r = jnp.clip(t - z, 0, chunks - 1) * depth
            at_l = jnp.clip(t - (n_chips - 1 - z), 0, chunks - 1) * depth
            send_r = lax.dynamic_slice_in_dim(start_r, at_r, depth, 0)
            send_l = lax.dynamic_slice_in_dim(start_l, at_l, depth, 0)
            if t > 0:
                send_r = (send_r + copy_columns(in_r, pass_r)).astype(jnp.bfloat16)
                send_l = (send_l + copy_columns(in_l, pass_l)).astype(jnp.bfloat16)
            in_r = lax.ppermute(send_r, "store", rightward)
            in_l = lax.ppermute(send_l, "store", leftward)
            if t == 3:
                in_r, base_values = lax.optimization_barrier((in_r, base_values))
            parts_r.append(copy_columns(in_r, take_r).astype(jnp.bfloat16))
            parts_l.append(copy_columns(in_l, take_l).astype(jnp.bfloat16))
        from_r = lax.dynamic_slice_in_dim(
            jnp.concatenate(parts_r, 0), jnp.clip(z - 1, 0, n_chips - 2) * depth, half, 0
        )
        from_l = lax.dynamic_slice_in_dim(
            jnp.concatenate(parts_l, 0), jnp.clip(n_chips - 2 - z, 0, n_chips - 2) * depth, half, 0
        )
        from_own = copy_columns(own, take_own).astype(jnp.bfloat16)
        found = from_own + jnp.where(z > 0, from_r, 0) + jnp.where(z < n_chips - 1, from_l, 0)
        here = found[:, wide:]
        there = lax.ppermute(found[:, :wide], "store", swap)
    low, high = jnp.where(first, here, there), jnp.where(first, there, here)
    cut = feats // 2
    inner = jnp.dot(tokens[:, :cut], low[:cut], preferred_element_type=jnp.float32)
    inner = inner + jnp.dot(tokens[:, cut:], high[:cut], preferred_element_type=jnp.float32)
    starts = exclusive_sum(lengths)
    row_ids = jnp.arange(rows, dtype=jnp.int32)
    inside = (starts[None, :] <= row_ids[:, None]) & (
        row_ids[:, None] < (starts + lengths)[None, :]
    )
    inner = jnp.sum(jnp.where(inside[:, :, None], inner.reshape(rows, n_seg, rank_cap), 0.0), axis=1)
    inner = exchange_sum(inner, n_tp)
    my_request = lax.dynamic_index_in_dim(all_requests, store, 0, keepdims=False)
    factors = column_gain(ranks, my_request, rank_cap)
    scaled = (inner[:, None, :] * factors[None, :, :]).astype(jnp.bfloat16)
    scaled = jnp.where(inside[:, :, None], scaled, 0).reshape(rows, wide)
    up_all = jnp.concatenate([low[cut:], high[cut:]], axis=0)
    delta = lax.dot_general(
        scaled, up_all, (((1,), (1,)), ((), ())), preferred_element_type=jnp.float32
    )
    return (base_values + delta).astype(jnp.bfloat16)


def share(x, axis, count):
    place, width = lax.axis_index(axis), 1
    while width < count:
        other = lax.ppermute(x, axis, [(i, i ^ width) for i in range(count)])
        low = (place // width) % 2 == 0
        x = jnp.concatenate([jnp.where(low, x, other), jnp.where(low, other, x)], axis=0)
        width *= 2
    return x


def before_hops(n_store, down, up):
    feats, outs, per_dev = down.shape[1], up.shape[2], down.shape[0]
    core = lax.rem(lax.axis_index("store"), 2)
    cut_d, cut_u = feats // 2, outs // 2
    swap = [(i, i ^ 1) for i in range(n_store)]

    def halves(which):
        return (
            lax.dynamic_slice_in_dim(down, which * cut_d, cut_d, 1),
            lax.dynamic_slice_in_dim(up, which * cut_u, cut_u, 2),
        )

    got_d, got_u = (lax.ppermute(x, "store", swap) for x in halves(1 - core))
    mine_d, mine_u = halves(core)
    up_rows = jnp.concatenate([x[a].T for x in (mine_u, got_u) for a in range(per_dev)], axis=1)
    return mine_d, got_d, up_rows


def whole_own(mine_d, got_d, up_rows):
    down_rows = jnp.concatenate([x[a] for x in (mine_d, got_d) for a in range(x.shape[0])], axis=1)
    return jnp.concatenate([down_rows, up_rows], axis=0)


def hop_kernel(
    n_chips, depth, tokens, value, mine_d, got_d, up_rows,
    own_r, own_l, pass_r, pass_l, take_own, take_r, take_l,
    here, there, near, arrived,
    own, give, far, out_r, out_l, in_r, in_l,
    sent_r, sent_l, came_r, came_l, sent_g, came_g, load_sem, far_sem,
):
    store, tp = lax.axis_index("store"), lax.axis_index("tp")
    z = store // 2
    sibling = store + 1 - 2 * (store % 2)
    chunks = own.shape[0] // depth
    wide, outs, pieces = here.shape[1], near.shape[1], 8
    piece = tokens.shape[1] // pieces
    per_dev, cut, rank_cap = mine_d.shape
    loads = [
        pltpu.make_async_copy(
            x.at[a],
            own.at[pl.ds(0, cut), pl.ds((i * per_dev + a) * rank_cap, rank_cap)],
            load_sem.at[i * per_dev + a],
        )
        for i, x in enumerate((mine_d, got_d))
        for a in range(per_dev)
    ]
    loads.append(
        pltpu.make_async_copy(
            up_rows, own.at[pl.ds(cut, own.shape[0] - cut), :], load_sem.at[2 * per_dev]
        )
    )
    for load in loads:
        load.start()
    far[...] = jnp.zeros_like(far)
    near[...] = jnp.zeros_like(near)
    right, left = z < n_chips - 1, z > 0
    barrier = pltpu.get_barrier_semaphore()

    @pl.when(right)
    def _():
        pl.semaphore_signal(
            barrier, inc=1, device_id={"store": store + 2}, device_id_type=pl.DeviceIdType.MESH
        )

    @pl.when(left)
    def _():
        pl.semaphore_signal(
            barrier, inc=1, device_id={"store": store - 2}, device_id_type=pl.DeviceIdType.MESH
        )

    for other in ({"store": sibling}, {"tp": 1 - tp}):
        pl.semaphore_signal(
            barrier, inc=1, device_id=other, device_id_type=pl.DeviceIdType.MESH
        )
    pl.semaphore_wait(barrier, 2 + right.astype(jnp.int32) + left.astype(jnp.int32))
    for load in loads:
        load.wait()

    streams = (
        (z, right, left, store + 2, own_r, pass_r, take_r, out_r, in_r, sent_r, came_r),
        (
            n_chips - 1 - z, left, right, store - 2,
            own_l, pass_l, take_l, out_l, in_l, sent_l, came_l,
        ),
    )

    def copy(stream, k):
        _, _, _, to, _, _, _, out, into, sent, came = stream
        rows = pl.ds(pl.multiple_of(k * depth, depth), depth)
        return pltpu.make_async_remote_copy(
            src_ref=out.at[rows, :],
            dst_ref=into.at[rows, :],
            send_sem=sent.at[k],
            recv_sem=came.at[k],
            device_id={"store": to},
            device_id_type=pl.DeviceIdType.MESH,
        )

    def hand_over(k):
        rows = pl.ds(pl.multiple_of(k * depth, depth), depth)
        return pltpu.make_async_remote_copy(
            src_ref=give.at[rows, :],
            dst_ref=there.at[rows, :],
            send_sem=sent_g.at[k],
            recv_sem=came_g.at[k],
            device_id={"store": sibling},
            device_id_type=pl.DeviceIdType.MESH,
        )

    send_far = pltpu.make_async_remote_copy(
        src_ref=far,
        dst_ref=arrived,
        send_sem=far_sem.at[0],
        recv_sem=far_sem.at[1],
        device_id={"tp": 1 - tp},
        device_id_type=pl.DeviceIdType.MESH,
    )

    def base_piece(total, i, column):
        inner = pl.ds(pl.multiple_of(i * piece, piece), piece)
        outer = pl.ds(pl.multiple_of(column, outs), outs)
        total[...] += copy_columns(tokens[:, inner], value[inner, outer])

    def step(t, carry):
        for stream in streams:
            order, gives, gets, _, start, onward, _, out, into, _, _ = stream
            k = t - 2 * order
            live = (k >= 0) & (k < chunks)

            @pl.when(live & gets)
            def _(stream=stream, k=k):
                copy(stream, k).wait_recv()

            @pl.when(live & gives & gets)
            def _(k=k, start=start, onward=onward, out=out, into=into):
                rows = pl.ds(pl.multiple_of(k * depth, depth), depth)
                moved = copy_columns(into[rows, :], onward[...])
                fresh = copy_columns(own[rows, :], start[...])
                out[rows, :] = (fresh + moved).astype(jnp.bfloat16)

            @pl.when(live & gives & jnp.logical_not(gets))
            def _(k=k, start=start, out=out):
                rows = pl.ds(pl.multiple_of(k * depth, depth), depth)
                out[rows, :] = copy_columns(own[rows, :], start[...]).astype(jnp.bfloat16)

            @pl.when(live & gives)
            def _(stream=stream, k=k):
                copy(stream, k).start()

        @pl.when(t < chunks)
        def _():
            rows = pl.ds(pl.multiple_of(t * depth, depth), depth)
            picked = copy_columns(own[rows, :], take_own[...]).astype(jnp.bfloat16)
            give[rows, :] = picked[:, :wide]
            here[rows, :] = picked[:, wide:]

        for stream in streams:
            order, _, gets, _, _, _, take, _, into, _, _ = stream
            k = t - 2 * order

            @pl.when((k >= 0) & (k < chunks) & gets)
            def _(k=k, take=take, into=into):
                rows = pl.ds(pl.multiple_of(k * depth, depth), depth)
                picked = copy_columns(into[rows, :], take[...]).astype(jnp.bfloat16)
                give[rows, :] = give[rows, :] + picked[:, :wide]
                here[rows, :] = here[rows, :] + picked[:, wide:]

        done = t - 2 * jnp.maximum(z, n_chips - 1 - z)

        @pl.when((done >= 0) & (done < chunks))
        def _():
            hand_over(done).start()

        @pl.when(t < pieces)
        def _():
            base_piece(far, t, (1 - tp) * outs)

        @pl.when(t == pieces)
        def _():
            send_far.start()

        @pl.when((t >= pieces) & (t < 2 * pieces))
        def _():
            base_piece(near, t - pieces, tp * outs)

        return carry

    lax.fori_loop(0, max(chunks + 2 * (n_chips - 1), 2 * pieces), step, 0)

    def finish(k, carry):
        for stream in streams:

            @pl.when(stream[1])
            def _(stream=stream):
                copy(stream, k).wait_send()

        hand_over(k).wait()
        return carry

    lax.fori_loop(0, chunks, finish, 0)
    send_far.wait()


def hop_call(identity, n_chips, outs, tokens, value, mine_d, got_d, up_rows, *chosen):
    own_width, capacity = chosen[0].shape
    half, wide = mine_d.shape[1] + up_rows.shape[0], chosen[4].shape[1] // 2
    depth = 128 if half % 128 == 0 else 16
    vmem, left_out = pl.BlockSpec(memory_space=pltpu.VMEM), pl.BlockSpec(memory_space=pl.ANY)
    line = pltpu.VMEM((half, capacity), jnp.bfloat16)
    marks = pltpu.SemaphoreType.DMA((half // depth,))
    sums = jax.ShapeDtypeStruct((tokens.shape[0], outs), jnp.float32)
    part = jax.ShapeDtypeStruct((half, wide), jnp.bfloat16)
    return pl.pallas_call(
        functools.partial(hop_kernel, n_chips, depth),
        out_shape=[part, part, sums, sums],
        in_specs=[vmem] * 2 + [left_out] * 3 + [vmem] * 7,
        out_specs=[vmem] * 4,
        scratch_shapes=[
            pltpu.VMEM((half, own_width), jnp.bfloat16),
            pltpu.VMEM(part.shape, part.dtype),
            pltpu.VMEM(sums.shape, sums.dtype),
        ]
        + [line] * 4
        + [marks] * 6
        + [
            pltpu.SemaphoreType.DMA((2 * mine_d.shape[0] + 1,)),
            pltpu.SemaphoreType.DMA((2,)),
        ],
        compiler_params=pltpu.CompilerParams(
            collective_id=identity, has_side_effects=True, vmem_limit_bytes=61 * 1024 * 1024
        ),
    )(tokens, value, mine_d, got_d, up_rows, *chosen)


def by_hops(n_grp, n_store, n_tp, tokens, value_matrix, down, up, rank_list, requests, lengths):
    n_chips, per_dev, rank_cap = n_store // 2, down.shape[0], down.shape[2]
    n_seg = requests.shape[1]
    n_adapters = n_store * per_dev
    store, grp = lax.axis_index("store"), lax.axis_index("grp")
    my_ranks = lax.dynamic_slice_in_dim(rank_list, store * per_dev, per_dev, 0)
    note = jnp.concatenate([requests[0], my_ranks])[None, :]
    notes = share(share(note, "store", n_store), "grp", n_grp)
    notes = notes.reshape(n_grp, n_store, n_seg + per_dev)
    ids = jnp.arange(n_adapters, dtype=jnp.int32)
    owner_chip = ids // (2 * per_dev)
    tables, load = [], 0
    for g in range(n_grp):
        asked = notes[g, :, :n_seg].reshape(n_chips, 2 * n_seg)
        asked = jnp.any(asked[:, :, None] == ids[None, None, :], axis=1)
        ranks = notes[g, :, n_seg:].reshape(n_adapters)
        right, left = link_tables(asked, ranks, n_chips, owner_chip)
        tables.append(jnp.stack([right, left]))
        load = jnp.maximum(load, jnp.max(jnp.sum(tables[-1], axis=-1)))
    mine = lax.dynamic_index_in_dim(jnp.stack(tables), grp, 0, keepdims=False)
    all_requests = lax.dynamic_index_in_dim(notes[:, :, :n_seg], grp, 0, keepdims=False)
    mine_d, got_d, up_rows = before_hops(n_store, down, up)
    most = n_chips * per_dev * rank_cap
    sizes = [most * part // 16 for part in CAPACITY_PARTS]
    branches = [
        functools.partial(
            hop_plan, size, n_store, n_tp, i if KERNEL and i + 1 < len(sizes) else None,
            rank_cap, up.shape[2],
        )
        for i, size in enumerate(sizes)
    ]
    branch = sum((load > size).astype(jnp.int32) for size in sizes[:-1])
    return lax.switch(
        branch, branches, tokens, value_matrix, mine_d, got_d, up_rows, rank_list, all_requests,
        lengths[0], mine[0], mine[1],
    )


def solution(mesh):
    in_specs = (
        P(("grp", "store"), "tp"),
        P("tp", None),
        P(("grp", "store"), "tp", None),
        P(("grp", "store"), None, "tp"),
        P("grp"),
        P(("grp", "store"), None),
        P(("grp", "store"), None),
    )
    out_specs = P(("grp", "store"), "tp")
    n_grp, n_store, n_tp = (mesh.shape[axis] for axis in ("grp", "store", "tp"))
    body = local
    if n_store % 2 == 0 and n_tp == 2 and n_store in (4, 8) and n_grp in (1, 2):
        body = functools.partial(by_hops, n_grp, n_store, n_tp)
    return jax.shard_map(body, mesh=mesh, in_specs=in_specs, out_specs=out_specs, check_vma=False)
```
